512 devices in a mesh: row: 16 (over z_hi, x), col: 32 (over z_lo, y, core).
Axes of the slice: x: 4, y: 4, z: 16 (z_hi: 4, z_lo: 4; z = z_hi * 4 + z_lo), core: 2. Of those that a mesh axis runs over, the one named last changes fastest.
Arguments:
- iterate: bfloat16 [3584, 18432], P('row', 'col'), may hold values from -0.046875 to 0.046875
Outputs:
- update: bfloat16 [3584, 18432], P('row', 'col')
The draws below stay inside these ranges and needn't reach their ends.
All inputs are finite; a program needn't handle non-finite values.
Results may differ from the reference program's by a relative error of at most 0.0089.
Values may be sent and summed in bfloat16 or wider, within the bound.
A program may use at most 64 MiB of HBM per device.

```python
import math
import jax
import jax.numpy as jnp

ROWS = 3584
COLS = 18432


def level_of(stream_key, extent, shards, low, largest):
    level, own = 1.0, jax.random.fold_in(stream_key, 6)
    for axis_at, parts in shards:
        draws = jnp.exp(jax.random.uniform(jax.random.fold_in(own, axis_at), (parts,), jnp.float32, low / len(shards), largest / len(shards)))
        level = level * jnp.repeat(draws, extent[axis_at] // parts).reshape([-1 if axis == axis_at else 1 for axis in range(len(extent))])
    return level


def bell_draw(stream_key, shape, deviation, most, split=(), kind=jnp.bfloat16):
    drawn = deviation * jax.random.normal(stream_key, shape, jnp.float32)
    if split:
        drawn = drawn * level_of(stream_key, shape, split, -0.22, 0.18)
    return jnp.clip(drawn, -most, most).astype(kind)


def setup_inputs(seed: int = 0) -> dict:
    arg_keys = jax.random.split(jax.random.key(seed), 2)
    iterate = bell_draw(arg_keys[0], (ROWS, COLS), COLS ** -0.5, 0.046875, ((0, 16), (1, 32)))
    return dict(iterate=iterate)


coeff_first = 3.4445
coeff_second = -4.775
coeff_third = 2.0315

def reference(iterate):
    gram = jnp.dot(iterate, iterate.T, preferred_element_type=jnp.float32).astype(jnp.bfloat16)
    square = jnp.dot(gram, gram, preferred_element_type=jnp.float32)
    poly = (coeff_second * gram.astype(jnp.float32) + coeff_third * square).astype(jnp.bfloat16)
    product = jnp.dot(poly, iterate, preferred_element_type=jnp.float32)
    factor = 0.2 * math.sqrt(max(ROWS, COLS))
    scaled = factor * (coeff_first * iterate.astype(jnp.float32) + product)
    return scaled.astype(jnp.bfloat16)
```

```python
import functools
import math

import jax
import jax.numpy as jnp
from jax import lax
from jax.experimental import pallas as pl
from jax.experimental.pallas import tpu as pltpu
from jax.sharding import PartitionSpec as P

MESH = pl.DeviceIdType.MESH
ROWS = 3584
COLS = 18432
R = 224
H = 112
K = 576
A = 896
Q = 32
bf16 = jnp.bfloat16
f32 = jnp.float32

coeff_first = 3.4445
coeff_second = -4.775
coeff_third = 2.0315
factor = 0.2 * math.sqrt(max(ROWS, COLS))

NT = (((1,), (1,)), ((), ()))
TN = (((0,), (0,)), ((), ()))


def dot(x, y, dims):
    return lax.dot_general(x, y, dims, preferred_element_type=f32)


def kernel(
    x_ref, o_ref, xa, xb, gk, gs, gr, yk, ys, yr, zk, zs, zr, mg, ng, pk, ps, pr, pt, uk, us, ur, ss, rs
):
    row, col = lax.axis_index("row"), lax.axis_index("col")
    a, b = row // 4, row % 4
    c, d, e = col // 8, (col // 2) % 4, col % 2
    f = 1 - e

    def at(a=a, b=b, c=c, d=d, e=e):
        return (a * 4 + b, c * 8 + d * 2 + e)

    def up(v, k):
        return (v + k) % 4

    barrier = pltpu.get_barrier_semaphore()
    friends = [at(e=f)]
    for k in range(1, 4):
        friends += [at(a=up(a, k)), at(b=up(b, k)), at(c=up(c, k)), at(d=up(d, k))]
    for friend in friends:
        pl.semaphore_signal(barrier, inc=1, device_id=friend, device_id_type=MESH)
    pl.semaphore_wait(barrier, len(friends))

    started = []
    count = [0]

    def send(src, dst, to, landing):
        n = count[0]
        count[0] += 1
        copy = pltpu.make_async_remote_copy(
            src_ref=src, dst_ref=dst, send_sem=ss.at[n], recv_sem=rs.at[n], device_id=to, device_id_type=MESH
        )
        copy.start()
        started.append(copy)
        return pltpu.make_async_remote_copy(
            src_ref=src, dst_ref=landing, send_sem=ss.at[n], recv_sem=rs.at[n], device_id=to, device_id_type=MESH
        )

    def xrows(v):
        return xa.at[pl.ds(pl.multiple_of(v * R, 16), R)]

    def half(h):
        return x_ref.at[pl.ds(h * H, H)]

    fwd0 = send(half(0), xb.at[0, a], at(a=up(a, 1)), xb.at[0, up(a, 3)])
    bwd1 = send(half(1), xb.at[1, a], at(a=up(a, 3)), xb.at[1, up(a, 1)])
    fwd1 = send(half(1), xb.at[1, a], at(a=up(a, 1)), xb.at[1, up(a, 3)])
    bwd0 = send(half(0), xb.at[0, a], at(a=up(a, 3)), xb.at[0, up(a, 1)])
    xin = [send(x_ref, xrows(b), at(b=up(b, k)), xrows(up(b, 4 - k))) for k in (1, 3, 2)]
    xa[pl.ds(pl.multiple_of(b * R, 16), R)] = x_ref[...]
    xb[0, a] = x_ref[:H]
    xb[1, a] = x_ref[H:]
    fwd0.wait_recv()
    far0 = send(xb.at[0, up(a, 3)], xb.at[0, up(a, 3)], at(a=up(a, 1)), xb.at[0, up(a, 2)])
    bwd1.wait_recv()
    far1 = send(xb.at[1, up(a, 1)], xb.at[1, up(a, 1)], at(a=up(a, 3)), xb.at[1, up(a, 2)])
    for copy in xin + [fwd1, bwd0, far0, far1]:
        copy.wait_recv()

    gs[...] = dot(xb[f].reshape(4 * H, K), xa[...], NT).astype(bf16).reshape(4, H, A)
    order = (1, 3, 2, 0)
    cin = {j: send(gs.at[up(d, j)], gr.at[up(d, j)], at(e=f), gr.at[up(d, j)]) for j in order}
    gk[...] = dot(xb[e].reshape(4 * H, K), xa[...], NT).reshape(4, H, A)
    yin = []
    for j in order:
        cin[j].wait_recv()
        if j:
            ys[j - 1] = (gk[up(d, j)] + gr[up(d, j)].astype(f32)).astype(bf16)
            yin.append(send(ys.at[j - 1], yr.at[j - 1], at(d=up(d, j)), yr.at[j - 1]))
        else:
            yk[:H] = gk[d] + gr[d].astype(f32)
    yk[H:] = jnp.zeros((4 * Q - H, A), f32)
    for copy in yin:
        copy.wait_recv()
    yk[:H] += yr[0].astype(f32) + yr[1].astype(f32) + yr[2].astype(f32)

    def part(v):
        return yk[pl.ds(pl.multiple_of(v * Q, Q), Q)]

    zin = []
    for j in (1, 2, 3):
        zs[j - 1] = part(up(c, j)).astype(bf16)
        zin.append(send(zs.at[j - 1], zr.at[j - 1], at(c=up(c, j)), zr.at[j - 1]))
    for copy in zin:
        copy.wait_recv()
    zk[...] = (part(c) + zr[0].astype(f32) + zr[1].astype(f32) + zr[2].astype(f32)).astype(bf16)

    min_ = [send(zk, mg.at[d, b], at(b=up(b, k)), mg.at[d, up(b, 4 - k)]) for k in (1, 3, 2)]
    nin = [send(zk, ng.at[e, c], at(c=up(c, k)), ng.at[e, up(c, 4 - k)]) for k in (1, 2, 3)]
    mg[d, b] = zk[...]
    ng[e, c] = zk[...]
    for copy in min_:
        copy.wait_recv()
    myin = [send(mg.at[d], mg.at[d], at(d=up(d, k)), mg.at[up(d, 4 - k)]) for k in (1, 3, 2)]
    for copy in nin:
        copy.wait_recv()
    ncore = send(ng.at[e], ng.at[e], at(e=f), ng.at[f])
    for copy in myin + [ncore]:
        copy.wait_recv()

    strips = mg[...].reshape(16 * Q, A)
    for h in range(2):
        first = lax.broadcasted_iota(jnp.int32, (H, A), 0) + (b * R + h * H)
        place = lax.broadcasted_iota(jnp.int32, (H, A), 1)
        hot = jnp.where((first == place) & (d == a), 1.0, 0.0).astype(bf16)
        left = ng[h].reshape(4 * Q, A)[:H]
        tile = coeff_third * dot(left, strips, NT) + coeff_second * dot(hot, strips, NT)
        for q in range(4):
            pk[q, h] = tile[:, q * 128 : (q + 1) * 128]
    pin = []
    for j in (1, 3, 2):
        ps[j - 1] = pk[up(a, j)].astype(bf16)
        pin.append(send(ps.at[j - 1], pr.at[j - 1], at(a=up(a, j)), pr.at[j - 1]))
    for copy in pin:
        copy.wait_recv()
    for h in range(2):
        pt[e, c, h, d] = (
            pk[a, h] + pr[0, h].astype(f32) + pr[1, h].astype(f32) + pr[2, h].astype(f32)
        ).astype(bf16)

    def tile_of(e, c, d):
        return pt.at[e, c, :, d]

    tin = {k: send(tile_of(e, c, d), tile_of(e, c, d), at(c=up(c, k)), tile_of(e, up(c, 4 - k), d)) for k in (1, 2, 3)}
    tyin = {}
    for k in (0, 1, 2, 3):
        src = up(c, 4 - k)
        if k:
            tin[k].wait_recv()
        tyin[k] = [
            send(tile_of(e, src, d), tile_of(e, src, d), at(d=up(d, j)), tile_of(e, src, up(d, 4 - j)))
            for j in (1, 3, 2)
        ]
    tcin = {}
    for k in (0, 1, 2, 3):
        src = up(c, 4 - k)
        for copy in tyin[k]:
            copy.wait_recv()
        tcin[k] = send(pt.at[e, src], pt.at[e, src], at(e=f), pt.at[f, src])

    right = [xb[h].reshape(4 * H, K) for h in range(2)]
    uin = []
    for g in range(2):
        w = e if g == 0 else f
        if g:
            for k in range(4):
                tcin[k].wait_recv()
        for q in range(4):
            u = dot(pt[w, q, 0].reshape(4 * H, 128), right[0], TN) + dot(pt[w, q, 1].reshape(4 * H, 128), right[1], TN)
            rows = min(Q, H - q * Q)
            for v in range(4):
                uk[v, w, q * Q : q * Q + rows] = u[v * Q : v * Q + rows]
        for j in (1, 3, 2):
            us[j - 1, w] = uk[up(b, j), w].astype(bf16)
            uin.append(send(us.at[j - 1, w], ur.at[j - 1, w], at(b=up(b, j)), ur.at[j - 1, w]))
    for copy in uin:
        copy.wait_recv()
    for h in range(2):
        total = uk[b, h] + ur[0, h].astype(f32) + ur[1, h].astype(f32) + ur[2, h].astype(f32)
        o_ref[h * H : (h + 1) * H] = (factor * (coeff_first * x_ref[h * H : (h + 1) * H].astype(f32) + total)).astype(bf16)
    for copy in started:
        copy.wait_send()


def step(x):
    vmem = pltpu.VMEM
    return pl.pallas_call(
        kernel,
        out_shape=jax.ShapeDtypeStruct((R, K), bf16),
        in_specs=[pl.BlockSpec(memory_space=vmem)],
        out_specs=pl.BlockSpec(memory_space=vmem),
        scratch_shapes=[
            vmem((A, K), bf16),
            vmem((2, 4, H, K), bf16),
            vmem((4, H, A), f32),
            vmem((4, H, A), bf16),
            vmem((4, H, A), bf16),
            vmem((4 * Q, A), f32),
            vmem((3, H, A), bf16),
            vmem((3, H, A), bf16),
            vmem((Q, A), bf16),
            vmem((3, Q, A), bf16),
            vmem((3, Q, A), bf16),
            vmem((4, 4, Q, A), bf16),
            vmem((2, 4, Q, A), bf16),
            vmem((4, 2, H, 128), f32),
            vmem((3, 2, H, 128), bf16),
            vmem((3, 2, H, 128), bf16),
            vmem((2, 4, 2, 4, H, 128), bf16),
            vmem((4, 2, H, K), f32),
            vmem((3, 2, H, K), bf16),
            vmem((3, 2, H, K), bf16),
            pltpu.SemaphoreType.DMA((64,)),
            pltpu.SemaphoreType.DMA((64,)),
        ],
        compiler_params=pltpu.CompilerParams(
            collective_id=0, has_side_effects=True, vmem_limit_bytes=44 << 20
        ),
        cost_estimate=pl.CostEstimate(flops=2 * 10**9, bytes_accessed=520000, transcendentals=0),
        name="newton_schulz",
    )(x)


def solution(mesh):
    return jax.shard_map(
        step, mesh=mesh, in_specs=(P("row", "col"),), out_specs=P("row", "col"), check_vma=False
    )
```

```python
import functools
import math

import jax
import jax.numpy as jnp
from jax import lax
from jax.experimental import pallas as pl
from jax.experimental.pallas import tpu as pltpu
from jax.sharding import PartitionSpec as P

MESH = pl.DeviceIdType.MESH
ROWS = 3584
COLS = 18432
R = 224
H = 112
K = 576
A = 896
Q = 32
bf16 = jnp.bfloat16
f32 = jnp.float32

coeff_first = 3.4445
coeff_second = -4.775
coeff_third = 2.0315
factor = 0.2 * math.sqrt(max(ROWS, COLS))

NN = (((1,), (0,)), ((), ()))
NT = (((1,), (1,)), ((), ()))


def dot(x, y, dims):
    return lax.dot_general(x, y, dims, preferred_element_type=f32)


def kernel(
    x_hbm,
    o_ref,
    x_ref,
    xp,
    ap,
    zp,
    xr,
    xa,
    gk,
    gs,
    gr,
    ys,
    yr,
    yk,
    zk,
    zs,
    zr,
    mg,
    ng,
    pk,
    ps,
    pr,
    pt,
    uk,
    ls,
    ss,
    rs,
):
    row, col = lax.axis_index("row"), lax.axis_index("col")
    a, b = row // 4, row % 4
    c, d, e = col // 8, (col // 2) % 4, col % 2
    f = 1 - e

    def at(a=a, b=b, c=c, d=d, e=e):
        return (a * 4 + b, c * 8 + d * 2 + e)

    def up(v, k):
        return (v + k) % 4

    fetch = pltpu.make_async_copy(x_hbm, x_ref, ls)
    fetch.start()

    barrier = pltpu.get_barrier_semaphore()
    friends = [at(e=f)]
    for k in range(1, 4):
        friends += [at(a=up(a, k)), at(b=up(b, k)), at(c=up(c, k)), at(d=up(d, k))]
    for friend in friends:
        pl.semaphore_signal(barrier, inc=1, device_id=friend, device_id_type=MESH)
    fetch.wait()
    xp[:, :K] = x_ref[:H]
    xp[:, K:] = x_ref[H:]
    pl.semaphore_wait(barrier, len(friends))

    started = []
    count = [4]

    def remote(src, dst, to, s, r):
        return pltpu.make_async_remote_copy(
            src_ref=src, dst_ref=dst, send_sem=ss.at[s], recv_sem=rs.at[r], device_id=to, device_id_type=MESH
        )

    def send(src, dst, to, landing):
        n = count[0]
        count[0] += 1
        copy = remote(src, dst, to, n, n)
        copy.start()
        started.append(copy)
        return remote(src, landing, to, n, n)

    piece = (pl.ds(0, 64), pl.ds(64, H - 64))
    up1, up3, far = up(a, 1), up(a, 3), up(a, 2)
    fwd, bwd = {}, {}
    for n in range(2):
        here = xp.at[piece[n]]
        fwd[n] = send(here, zp.at[a, piece[n]], at(a=up1), zp.at[up3, piece[n]])
        here = xp.at[piece[1 - n]]
        bwd[1 - n] = send(here, zp.at[a, piece[1 - n]], at(a=up3), zp.at[up1, piece[1 - n]])

    def over_x(src, plane):
        return {k: send(src, ap.at[plane, b], at(b=up(b, k)), ap.at[plane, up(b, 4 - k)]) for k in (1, 3, 2)}

    xin = {0: over_x(xp, a)}

    xr[:, :, :, H:] = jnp.zeros((4, 2, 4, 4 * Q - H, K), bf16)
    gk[:, 3, 16:] = jnp.zeros((4, 16, A), f32)
    ys[:, 3, 16:] = jnp.zeros((4, 16, A), bf16)

    def spread(packed, plane, place):
        xr[plane, 0, place, :H] = packed[:, :K]
        xr[plane, 1, place, :H] = packed[:, K:]

    def arrived(n, plane):
        for k in (1, 3, 2):
            xin[n][k].wait_recv()
            spread(ap[plane, up(b, 4 - k)], plane, up(b, 4 - k))

    for h in range(2):
        xr[a, h, b, :H] = x_ref[h * H : (h + 1) * H]
    arrived(0, a)
    for v in range(4):
        for h in range(2):
            xa[v, h] = xr[a, h, v, :H]

    cin, yin = {}, {}

    def gram(n, strip):
        right = xa[...].reshape(A, K)
        gs[strip] = dot(xr[strip, f, b, :H], right, NT).astype(bf16)
        cin[n] = send(gs.at[strip], gr.at[strip], at(e=f), gr.at[strip])
        part = dot(xr[strip, e, b, :H], right, NT)
        for j in range(4):
            size = min(Q, H - j * Q)
            gk[strip, j, :size] = part[j * Q : j * Q + size]

    def combine(n, strip):
        cin[n].wait_recv()
        for j in range(4):
            size = min(Q, H - j * Q)
            both = gk[strip, j, :size] + gr[strip, j * Q : j * Q + size].astype(f32)
            gk[strip, j, :size] = both
            ys[strip, j, :size] = both.astype(bf16)
        yin[n] = [
            send(ys.at[strip, up(d, k)], yr.at[strip, d], at(d=up(d, k)), yr.at[strip, up(d, 4 - k)]) for k in (1, 3, 2)
        ]

    def hand(strip):
        return remote(zs.at[strip], zr.at[c], at(c=strip), strip, c)

    def pass_on(n, strip):
        for copy in yin[n]:
            copy.wait_recv()
        total = gk[strip, d] + sum(yr[strip, up(d, k)].astype(f32) for k in (1, 2, 3))

        @pl.when(strip == c)
        def _():
            yk[...] = total

        @pl.when(strip != c)
        def _():
            zs[strip] = total.astype(bf16)
            hand(strip).start()

    gram(0, a)
    fwd[0].wait_recv()
    far0 = send(zp.at[up3, piece[0]], zp.at[up3, piece[0]], at(a=up1), zp.at[far, piece[0]])
    bwd[1].wait_recv()
    far1 = send(zp.at[up1, piece[1]], zp.at[up1, piece[1]], at(a=up3), zp.at[far, piece[1]])
    combine(0, a)
    fwd[1].wait_recv()
    xin[1] = over_x(zp.at[up3], up3)
    spread(zp[up3], up3, b)
    gram(1, up3)
    bwd[0].wait_recv()
    xin[2] = over_x(zp.at[up1], up1)
    spread(zp[up1], up1, b)
    gram(2, up1)
    combine(1, up3)
    combine(2, up1)
    pass_on(0, a)
    far0.wait_recv()
    far1.wait_recv()
    spread(zp[far], far, b)
    gram(3, far)
    xin[3] = over_x(zp.at[far], far)
    combine(3, far)
    pass_on(1, up3)
    pass_on(2, up1)
    pass_on(3, far)
    for k in (1, 2, 3):
        remote(zs.at[c], zr.at[up(c, k)], at(c=up(c, k)), c, up(c, k)).wait_recv()
    zk[...] = (yk[...] + sum(zr[up(c, k)].astype(f32) for k in (1, 2, 3))).astype(bf16)

    top, low = pl.ds(0, 16), pl.ds(16, 16)
    min_ = [send(zk.at[top], mg.at[b, d, top], at(b=up(b, k)), mg.at[up(b, 4 - k), d, top]) for k in (1, 3, 2)]
    myin = [send(zk.at[low], mg.at[b, d, low], at(d=up(d, k)), mg.at[b, up(d, 4 - k), low]) for k in (1, 3, 2)]
    nin = [send(zk, ng.at[c, e], at(c=up(c, k)), ng.at[up(c, 4 - k), e]) for k in (1, 2, 3)]
    mg[b, d] = zk[...]
    ng[c, e] = zk[...]
    for copy in min_:
        copy.wait_recv()
    m2in = [send(mg.at[:, d, top], mg.at[:, d, top], at(d=up(d, k)), mg.at[:, up(d, 4 - k), top]) for k in (1, 3, 2)]
    for copy in myin:
        copy.wait_recv()
    m2in += [send(mg.at[b, :, low], mg.at[b, :, low], at(b=up(b, k)), mg.at[up(b, 4 - k), :, low]) for k in (1, 3, 2)]
    for copy in nin:
        copy.wait_recv()
    ncore = send(ng.at[:, e], ng.at[:, e], at(e=f), ng.at[:, f])
    for copy in m2in + [ncore]:
        copy.wait_recv()

    strips = mg[...].reshape(16 * Q, A)
    pk[...] = (coeff_third * dot(ng[...].reshape(8 * Q, A), strips, NT)).reshape(4, 2 * Q, 16 * Q)
    pin = []
    for j in (1, 3, 2):
        ps[j - 1] = pk[up(a, j)].astype(bf16)
        pin.append(send(ps.at[j - 1], pr.at[j - 1], at(a=up(a, j)), pr.at[j - 1]))
    want = lax.broadcasted_iota(jnp.int32, (2 * Q, A), 0)
    place = lax.broadcasted_iota(jnp.int32, (2 * Q, A), 1)
    inside = want % Q
    hot = (place == b * R + (want // Q) * H + d * Q + inside) & (inside < H - d * Q)
    hot = jnp.where(hot, 1.0, 0.0).astype(bf16)
    own = pk[a] + coeff_second * dot(hot, strips, NT)
    arrived(1, up3)
    arrived(2, up1)
    arrived(3, far)
    for copy in pin:
        copy.wait_recv()
    pt[c, e, d] = (own + pr[0].astype(f32) + pr[1].astype(f32) + pr[2].astype(f32)).astype(bf16)

    def tile_of(c, d):
        return pt.at[c, e, d]

    tin = {k: send(tile_of(c, d), tile_of(c, d), at(c=up(c, k)), tile_of(up(c, 4 - k), d)) for k in (1, 2, 3)}
    tyin = {}
    for k in (0, 1, 2, 3):
        src = up(c, 4 - k)
        if k:
            tin[k].wait_recv()
        tyin[k] = [
            send(tile_of(src, d), tile_of(src, d), at(d=up(d, j)), tile_of(src, up(d, 4 - j))) for j in (1, 3, 2)
        ]

    def product(z, h):
        return dot(pt[z, h].reshape(8 * Q, 16 * Q), xr[z, h].reshape(16 * Q, K), NN)

    tcin = {}
    for k in (0, 1, 2, 3):
        src = up(c, 4 - k)
        for copy in tyin[k]:
            copy.wait_recv()
        tcin[k] = send(pt.at[src, e], pt.at[src, e], at(e=f), pt.at[src, f])
        if k:
            uk[...] += product(src, e)
            tcin[k - 1].wait_recv()
            uk[...] += product(up(c, 5 - k), f)
        else:
            uk[...] = product(src, e)
    tcin[3].wait_recv()
    uk[...] += product(up(c, 1), f)
    for h in range(2):
        for j in range(4):
            size = min(Q, H - j * Q)
            rows = slice(h * H + j * Q, h * H + j * Q + size)
            total = uk[(j * 2 + h) * Q : (j * 2 + h) * Q + size]
            o_ref[rows] = (factor * (coeff_first * x_ref[rows].astype(f32) + total)).astype(bf16)
    for copy in started:
        copy.wait_send()
    for strip in range(4):

        @pl.when(c != strip)
        def _():
            hand(strip).wait_send()


def step(x):
    vmem = pltpu.VMEM
    return pl.pallas_call(
        kernel,
        out_shape=jax.ShapeDtypeStruct((R, K), bf16),
        in_specs=[pl.BlockSpec(memory_space=pl.ANY)],
        out_specs=pl.BlockSpec(memory_space=vmem),
        scratch_shapes=[
            vmem((R, K), bf16),
            vmem((H, 2 * K), bf16),
            vmem((4, 4, H, 2 * K), bf16),
            vmem((4, H, 2 * K), bf16),
            vmem((4, 2, 4, 4 * Q, K), bf16),
            vmem((4, 2, H, K), bf16),
            vmem((4, 4, Q, A), f32),
            vmem((4, H, A), bf16),
            vmem((4, H, A), bf16),
            vmem((4, 4, Q, A), bf16),
            vmem((4, 4, Q, A), bf16),
            vmem((Q, A), f32),
            vmem((Q, A), bf16),
            vmem((4, Q, A), bf16),
            vmem((4, Q, A), bf16),
            vmem((4, 4, Q, A), bf16),
            vmem((4, 2, Q, A), bf16),
            vmem((4, 2 * Q, 16 * Q), f32),
            vmem((3, 2 * Q, 16 * Q), bf16),
            vmem((3, 2 * Q, 16 * Q), bf16),
            vmem((4, 2, 4, 2 * Q, 16 * Q), bf16),
            vmem((8 * Q, K), f32),
            pltpu.SemaphoreType.DMA,
            pltpu.SemaphoreType.DMA((128,)),
            pltpu.SemaphoreType.DMA((128,)),
        ],
        compiler_params=pltpu.CompilerParams(
            collective_id=0, has_side_effects=True, vmem_limit_bytes=60 << 20
        ),
        cost_estimate=pl.CostEstimate(flops=2 * 10**9, bytes_accessed=520000, transcendentals=0),
        name="newton_schulz",
    )(x)


def solution(mesh):
    return jax.shard_map(
        step, mesh=mesh, in_specs=(P("row", "col"),), out_specs=P("row", "col"), check_vma=False
    )
```

```python
import functools
import math

import jax
import jax.numpy as jnp
from jax import lax
from jax.experimental import pallas as pl
from jax.experimental.pallas import tpu as pltpu
from jax.sharding import PartitionSpec as P

MESH = pl.DeviceIdType.MESH
ROWS = 3584
COLS = 18432
R = 224
H = 112
K = 576
A = 896
Q = 32
bf16 = jnp.bfloat16
f32 = jnp.float32

coeff_first = 3.4445
coeff_second = -4.775
coeff_third = 2.0315
factor = 0.2 * math.sqrt(max(ROWS, COLS))

NN = (((1,), (0,)), ((), ()))
NT = (((1,), (1,)), ((), ()))


def dot(x, y, dims):
    return lax.dot_general(x, y, dims, preferred_element_type=f32)


def kernel(
    x_hbm,
    o_ref,
    x_ref,
    xp,
    ap,
    zp,
    xr,
    xa,
    gk,
    gs,
    gr,
    ys,
    yr,
    yk,
    zk,
    zs,
    zr,
    mg,
    ng,
    pk,
    ps,
    pr,
    pt,
    uk,
    ls,
    ss,
    rs,
):
    row, col = lax.axis_index("row"), lax.axis_index("col")
    a, b = row // 4, row % 4
    c, d, e = col // 8, (col // 2) % 4, col % 2
    f = 1 - e

    def at(a=a, b=b, c=c, d=d, e=e):
        return (a * 4 + b, c * 8 + d * 2 + e)

    def up(v, k):
        return (v + k) % 4

    fetch = pltpu.make_async_copy(x_hbm, x_ref, ls)
    fetch.start()

    barrier = pltpu.get_barrier_semaphore()
    friends = [at(e=f)]
    for k in range(1, 4):
        friends += [at(a=up(a, k)), at(b=up(b, k)), at(c=up(c, k)), at(d=up(d, k))]
    for friend in friends:
        pl.semaphore_signal(barrier, inc=1, device_id=friend, device_id_type=MESH)
    fetch.wait()
    xp[:, :K] = x_ref[:H]
    xp[:, K:] = x_ref[H:]
    pl.semaphore_wait(barrier, len(friends))

    started = []
    count = [4]

    def remote(src, dst, to, s, r):
        return pltpu.make_async_remote_copy(
            src_ref=src, dst_ref=dst, send_sem=ss.at[s], recv_sem=rs.at[r], device_id=to, device_id_type=MESH
        )

    def send(src, dst, to, landing):
        n = count[0]
        count[0] += 1
        copy = remote(src, dst, to, n, n)
        copy.start()
        started.append(copy)
        return remote(src, landing, to, n, n)

    piece = (pl.ds(0, 64), pl.ds(64, H - 64))
    up1, up3, far = up(a, 1), up(a, 3), up(a, 2)
    fwd, bwd = {}, {}
    for n in range(2):
        here = xp.at[piece[n]]
        fwd[n] = send(here, zp.at[a, piece[n]], at(a=up1), zp.at[up3, piece[n]])
        here = xp.at[piece[1 - n]]
        bwd[1 - n] = send(here, zp.at[a, piece[1 - n]], at(a=up3), zp.at[up1, piece[1 - n]])

    def over_x(src, plane):
        return {k: send(src, ap.at[plane, b], at(b=up(b, k)), ap.at[plane, up(b, 4 - k)]) for k in (1, 3, 2)}

    xin = {0: over_x(xp, a)}

    xr[:, :, :, H:] = jnp.zeros((4, 2, 4, 4 * Q - H, K), bf16)
    gk[:, 3, 16:] = jnp.zeros((4, 16, A), f32)
    ys[:, 3, 16:] = jnp.zeros((4, 16, A), bf16)

    def spread(packed, plane, place):
        xr[plane, 0, place, :H] = packed[:, :K]
        xr[plane, 1, place, :H] = packed[:, K:]

    def arrived(n, plane):
        for k in (1, 3, 2):
            xin[n][k].wait_recv()
            spread(ap[plane, up(b, 4 - k)], plane, up(b, 4 - k))

    for h in range(2):
        xr[a, h, b, :H] = x_ref[h * H : (h + 1) * H]
    arrived(0, a)
    for v in range(4):
        for h in range(2):
            xa[v, h] = xr[a, h, v, :H]

    cin, yin = {}, {}

    def gram(n, strip):
        right = xa[...].reshape(A, K)
        gs[strip] = dot(xr[strip, f, b, :H], right, NT).astype(bf16)
        cin[n] = send(gs.at[strip], gr.at[strip], at(e=f), gr.at[strip])
        part = dot(xr[strip, e, b, :H], right, NT)
        for j in range(4):
            size = min(Q, H - j * Q)
            gk[strip, j, :size] = part[j * Q : j * Q + size]

    def combine(n, strip):
        cin[n].wait_recv()
        for j in range(4):
            size = min(Q, H - j * Q)
            both = gk[strip, j, :size] + gr[strip, j * Q : j * Q + size].astype(f32)
            gk[strip, j, :size] = both
            ys[strip, j, :size] = both.astype(bf16)
        yin[n] = [
            send(ys.at[strip, up(d, k)], yr.at[strip, d], at(d=up(d, k)), yr.at[strip, up(d, 4 - k)]) for k in (1, 3, 2)
        ]

    def hand(strip):
        return remote(zs.at[strip], zr.at[c], at(c=strip), strip, c)

    def pass_on(n, strip):
        for copy in yin[n]:
            copy.wait_recv()
        total = gk[strip, d] + sum(yr[strip, up(d, k)].astype(f32) for k in (1, 2, 3))

        @pl.when(strip == c)
        def _():
            yk[...] = total

        @pl.when(strip != c)
        def _():
            zs[strip] = total.astype(bf16)
            hand(strip).start()

    gram(0, a)
    fwd[0].wait_recv()
    far0 = send(zp.at[up3, piece[0]], zp.at[up3, piece[0]], at(a=up1), zp.at[far, piece[0]])
    bwd[1].wait_recv()
    far1 = send(zp.at[up1, piece[1]], zp.at[up1, piece[1]], at(a=up3), zp.at[far, piece[1]])
    combine(0, a)
    fwd[1].wait_recv()
    xin[1] = over_x(zp.at[up3], up3)
    spread(zp[up3], up3, b)
    gram(1, up3)
    bwd[0].wait_recv()
    spread(zp[up1], up1, b)
    gram(2, up1)
    combine(1, up3)
    combine(2, up1)
    pass_on(0, a)
    far0.wait_recv()
    far1.wait_recv()
    spread(zp[far], far, b)
    gram(3, far)
    combine(3, far)
    pass_on(1, up3)
    pass_on(2, up1)
    pass_on(3, far)
    for k in (1, 2, 3):
        remote(zs.at[c], zr.at[up(c, k)], at(c=up(c, k)), c, up(c, k)).wait_recv()
    zk[...] = (yk[...] + sum(zr[up(c, k)].astype(f32) for k in (1, 2, 3))).astype(bf16)

    top, low = pl.ds(0, 16), pl.ds(16, 16)
    min_ = [send(zk.at[top], mg.at[b, d, top], at(b=up(b, k)), mg.at[up(b, 4 - k), d, top]) for k in (1, 3, 2)]
    myin = [send(zk.at[low], mg.at[b, d, low], at(d=up(d, k)), mg.at[b, up(d, 4 - k), low]) for k in (1, 3, 2)]
    nin = [send(zk, ng.at[c, e], at(c=up(c, k)), ng.at[up(c, 4 - k), e]) for k in (1, 2, 3)]
    mg[b, d] = zk[...]
    ng[c, e] = zk[...]
    for copy in min_:
        copy.wait_recv()
    m2in = [send(mg.at[:, d, top], mg.at[:, d, top], at(d=up(d, k)), mg.at[:, up(d, 4 - k), top]) for k in (1, 3, 2)]
    for copy in myin:
        copy.wait_recv()
    m2in += [send(mg.at[b, :, low], mg.at[b, :, low], at(b=up(b, k)), mg.at[up(b, 4 - k), :, low]) for k in (1, 3, 2)]
    for copy in nin:
        copy.wait_recv()
    ncore = send(ng.at[:, e], ng.at[:, e], at(e=f), ng.at[:, f])
    for copy in m2in + [ncore]:
        copy.wait_recv()

    strips = mg[...].reshape(16 * Q, A)
    pk[...] = (coeff_third * dot(ng[...].reshape(8 * Q, A), strips, NT)).reshape(4, 2 * Q, 16 * Q)
    pin = []
    for j in (1, 3, 2):
        ps[j - 1] = pk[up(a, j)].astype(bf16)
        pin.append(send(ps.at[j - 1], pr.at[j - 1], at(a=up(a, j)), pr.at[j - 1]))
    xin[2] = over_x(zp.at[up1], up1)
    xin[3] = over_x(zp.at[far], far)
    want = lax.broadcasted_iota(jnp.int32, (2 * Q, A), 0)
    place = lax.broadcasted_iota(jnp.int32, (2 * Q, A), 1)
    inside = want % Q
    hot = (place == b * R + (want // Q) * H + d * Q + inside) & (inside < H - d * Q)
    hot = jnp.where(hot, 1.0, 0.0).astype(bf16)
    own = pk[a] + coeff_second * dot(hot, strips, NT)
    arrived(1, up3)
    for copy in pin:
        copy.wait_recv()
    pt[c, e, d] = (own + pr[0].astype(f32) + pr[1].astype(f32) + pr[2].astype(f32)).astype(bf16)

    def tile_of(c, d):
        return pt.at[c, e, d]

    tin = {k: send(tile_of(c, d), tile_of(c, d), at(c=up(c, k)), tile_of(up(c, 4 - k), d)) for k in (1, 2, 3)}
    tyin = {}
    for k in (0, 1, 2, 3):
        src = up(c, 4 - k)
        if k:
            tin[k].wait_recv()
        tyin[k] = [
            send(tile_of(src, d), tile_of(src, d), at(d=up(d, j)), tile_of(src, up(d, 4 - j))) for j in (1, 3, 2)
        ]

    def product(z, h):
        return dot(pt[z, h].reshape(8 * Q, 16 * Q), xr[z, h].reshape(16 * Q, K), NN)

    arrived(2, up1)
    arrived(3, far)
    tcin = {}
    for k in (0, 1, 2, 3):
        src = up(c, 4 - k)
        for copy in tyin[k]:
            copy.wait_recv()
        tcin[k] = send(pt.at[src, e], pt.at[src, e], at(e=f), pt.at[src, f])
        if k:
            uk[...] += product(src, e)
            tcin[k - 1].wait_recv()
            uk[...] += product(up(c, 5 - k), f)
        else:
            uk[...] = product(src, e)
    tcin[3].wait_recv()
    uk[...] += product(up(c, 1), f)
    for h in range(2):
        for j in range(4):
            size = min(Q, H - j * Q)
            rows = slice(h * H + j * Q, h * H + j * Q + size)
            total = uk[(j * 2 + h) * Q : (j * 2 + h) * Q + size]
            o_ref[rows] = (factor * (coeff_first * x_ref[rows].astype(f32) + total)).astype(bf16)
    for copy in started:
        copy.wait_send()
    for strip in range(4):

        @pl.when(c != strip)
        def _():
            hand(strip).wait_send()


def step(x):
    vmem = pltpu.VMEM
    return pl.pallas_call(
        kernel,
        out_shape=jax.ShapeDtypeStruct((R, K), bf16),
        in_specs=[pl.BlockSpec(memory_space=pltpu.HBM)],
        out_specs=pl.BlockSpec(memory_space=vmem),
        scratch_shapes=[
            vmem((R, K), bf16),
            vmem((H, 2 * K), bf16),
            vmem((4, 4, H, 2 * K), bf16),
            vmem((4, H, 2 * K), bf16),
            vmem((4, 2, 4, 4 * Q, K), bf16),
            vmem((4, 2, H, K), bf16),
            vmem((4, 4, Q, A), f32),
            vmem((4, H, A), bf16),
            vmem((4, H, A), bf16),
            vmem((4, 4, Q, A), bf16),
            vmem((4, 4, Q, A), bf16),
            vmem((Q, A), f32),
            vmem((Q, A), bf16),
            vmem((4, Q, A), bf16),
            vmem((4, Q, A), bf16),
            vmem((4, 4, Q, A), bf16),
            vmem((4, 2, Q, A), bf16),
            vmem((4, 2 * Q, 16 * Q), f32),
            vmem((3, 2 * Q, 16 * Q), bf16),
            vmem((3, 2 * Q, 16 * Q), bf16),
            vmem((4, 2, 4, 2 * Q, 16 * Q), bf16),
            vmem((8 * Q, K), f32),
            pltpu.SemaphoreType.DMA,
            pltpu.SemaphoreType.DMA((128,)),
            pltpu.SemaphoreType.DMA((128,)),
        ],
        compiler_params=pltpu.CompilerParams(
            collective_id=0, has_side_effects=True, vmem_limit_bytes=44 << 20
        ),
        cost_estimate=pl.CostEstimate(flops=2 * 10**9, bytes_accessed=520000, transcendentals=0),
        name="newton_schulz",
    )(x)


def solution(mesh):
    return jax.shard_map(
        step, mesh=mesh, in_specs=(P("row", "col"),), out_specs=P("row", "col"), check_vma=False
    )
```

```python
import functools
import math

import jax
import jax.numpy as jnp
from jax import lax
from jax.experimental import pallas as pl
from jax.experimental.pallas import tpu as pltpu
from jax.sharding import PartitionSpec as P

MESH = pl.DeviceIdType.MESH
ROWS = 3584
COLS = 18432
R = 224
H = 112
K = 576
A = 896
Q = 32
bf16 = jnp.bfloat16
f32 = jnp.float32

coeff_first = 3.4445
coeff_second = -4.775
coeff_third = 2.0315
factor = 0.2 * math.sqrt(max(ROWS, COLS))

NN = (((1,), (0,)), ((), ()))
NT = (((1,), (1,)), ((), ()))


def dot(x, y, dims):
    return lax.dot_general(x, y, dims, preferred_element_type=f32)


def kernel(
    x_hbm,
    o_ref,
    x_ref,
    xp,
    ap,
    zp,
    xr,
    xa,
    gk,
    gs,
    gr,
    ys,
    yr,
    yk,
    zk,
    zs,
    zr,
    mg,
    ng,
    ps,
    pr,
    pt,
    uk,
    ls,
    ss,
    rs,
):
    row, col = lax.axis_index("row"), lax.axis_index("col")
    a, b = row // 4, row % 4
    c, d, e = col // 8, (col // 2) % 4, col % 2
    f = 1 - e

    def at(a=a, b=b, c=c, d=d, e=e):
        return (a * 4 + b, c * 8 + d * 2 + e)

    def up(v, k):
        return (v + k) % 4

    fetch = pltpu.make_async_copy(x_hbm, x_ref, ls)
    fetch.start()

    barrier = pltpu.get_barrier_semaphore()
    friends = [at(e=f)]
    for k in range(1, 4):
        friends += [at(a=up(a, k)), at(b=up(b, k)), at(c=up(c, k)), at(d=up(d, k))]
    for friend in friends:
        pl.semaphore_signal(barrier, inc=1, device_id=friend, device_id_type=MESH)
    fetch.wait()
    xp[:, :K] = x_ref[:H]
    xp[:, K:] = x_ref[H:]
    pl.semaphore_wait(barrier, len(friends))

    started = []
    count = [4]

    def remote(src, dst, to, s, r):
        return pltpu.make_async_remote_copy(
            src_ref=src, dst_ref=dst, send_sem=ss.at[s], recv_sem=rs.at[r], device_id=to, device_id_type=MESH
        )

    def send(src, dst, to, landing):
        n = count[0]
        count[0] += 1
        copy = remote(src, dst, to, n, n)
        copy.start()
        started.append(copy)
        return remote(src, landing, to, n, n)

    piece = (pl.ds(0, 64), pl.ds(64, H - 64))
    up1, up3, far = up(a, 1), up(a, 3), up(a, 2)
    fwd, bwd = {}, {}
    for n in range(2):
        here = xp.at[piece[n]]
        fwd[n] = send(here, zp.at[a, piece[n]], at(a=up1), zp.at[up3, piece[n]])
        here = xp.at[piece[1 - n]]
        bwd[1 - n] = send(here, zp.at[a, piece[1 - n]], at(a=up3), zp.at[up1, piece[1 - n]])

    def over_x(src, plane):
        return {k: send(src, ap.at[plane, b], at(b=up(b, k)), ap.at[plane, up(b, 4 - k)]) for k in (1, 3, 2)}

    xin = {0: over_x(xp, a)}

    xr[:, :, :, H:] = jnp.zeros((4, 2, 4, 4 * Q - H, K), bf16)
    gk[:, 3, 16:] = jnp.zeros((4, 16, A), f32)
    ys[:, 3, 16:] = jnp.zeros((4, 16, A), bf16)

    def spread(packed, plane, place):
        xr[plane, 0, place, :H] = packed[:, :K]
        xr[plane, 1, place, :H] = packed[:, K:]

    def arrived(n, plane):
        for k in (1, 3, 2):
            xin[n][k].wait_recv()
            spread(ap[plane, up(b, 4 - k)], plane, up(b, 4 - k))

    for h in range(2):
        xr[a, h, b, :H] = x_ref[h * H : (h + 1) * H]
    arrived(0, a)
    for v in range(4):
        for h in range(2):
            xa[v, h] = xr[a, h, v, :H]

    cin, yin = {}, {}

    def gram(n, strip):
        right = xa[...].reshape(A, K)
        gs[strip] = dot(xr[strip, f, b, :H], right, NT).astype(bf16)
        cin[n] = send(gs.at[strip], gr.at[strip], at(e=f), gr.at[strip])
        part = dot(xr[strip, e, b, :H], right, NT)
        for j in range(4):
            size = min(Q, H - j * Q)
            gk[strip, j, :size] = part[j * Q : j * Q + size]

    def combine(n, strip):
        cin[n].wait_recv()
        for j in range(4):
            size = min(Q, H - j * Q)
            both = gk[strip, j, :size] + gr[strip, j * Q : j * Q + size].astype(f32)
            gk[strip, j, :size] = both
            ys[strip, j, :size] = both.astype(bf16)
        yin[n] = [
            send(ys.at[strip, up(d, k)], yr.at[strip, d], at(d=up(d, k)), yr.at[strip, up(d, 4 - k)]) for k in (1, 3, 2)
        ]

    def hand(strip):
        return remote(zs.at[strip], zr.at[c], at(c=strip), strip, c)

    def pass_on(n, strip):
        for copy in yin[n]:
            copy.wait_recv()
        total = gk[strip, d] + sum(yr[strip, up(d, k)].astype(f32) for k in (1, 2, 3))

        @pl.when(strip == c)
        def _():
            yk[...] = total

        @pl.when(strip != c)
        def _():
            zs[strip] = total.astype(bf16)
            hand(strip).start()

    gram(0, a)
    fwd[0].wait_recv()
    far0 = send(zp.at[up3, piece[0]], zp.at[up3, piece[0]], at(a=up1), zp.at[far, piece[0]])
    bwd[1].wait_recv()
    far1 = send(zp.at[up1, piece[1]], zp.at[up1, piece[1]], at(a=up3), zp.at[far, piece[1]])
    combine(0, a)
    fwd[1].wait_recv()
    xin[1] = over_x(zp.at[up3], up3)
    spread(zp[up3], up3, b)
    gram(1, up3)
    bwd[0].wait_recv()
    spread(zp[up1], up1, b)
    gram(2, up1)
    combine(1, up3)
    combine(2, up1)
    pass_on(0, a)
    far0.wait_recv()
    far1.wait_recv()
    spread(zp[far], far, b)
    gram(3, far)
    combine(3, far)
    pass_on(1, up3)
    pass_on(2, up1)
    pass_on(3, far)
    for k in (1, 2, 3):
        remote(zs.at[c], zr.at[up(c, k)], at(c=up(c, k)), c, up(c, k)).wait_recv()
    zk[...] = (yk[...] + sum(zr[up(c, k)].astype(f32) for k in (1, 2, 3))).astype(bf16)

    top, low = pl.ds(0, 16), pl.ds(16, 16)
    min_ = [send(zk.at[top], mg.at[b, d, top], at(b=up(b, k)), mg.at[up(b, 4 - k), d, top]) for k in (1, 3, 2)]
    myin = [send(zk.at[low], mg.at[b, d, low], at(d=up(d, k)), mg.at[b, up(d, 4 - k), low]) for k in (1, 3, 2)]
    nin = [send(zk, ng.at[c, e], at(c=up(c, k)), ng.at[up(c, 4 - k), e]) for k in (1, 2, 3)]
    mg[b, d] = zk[...]
    ng[c, e] = zk[...]
    for copy in min_:
        copy.wait_recv()
    m2in = [send(mg.at[:, d, top], mg.at[:, d, top], at(d=up(d, k)), mg.at[:, up(d, 4 - k), top]) for k in (1, 3, 2)]
    for copy in myin:
        copy.wait_recv()
    m2in += [send(mg.at[b, :, low], mg.at[b, :, low], at(b=up(b, k)), mg.at[up(b, 4 - k), :, low]) for k in (1, 3, 2)]
    for copy in nin:
        copy.wait_recv()
    ncore = send(ng.at[:, e], ng.at[:, e], at(e=f), ng.at[:, f])
    for copy in m2in + [ncore]:
        copy.wait_recv()

    strips = mg[...].reshape(16 * Q, A)
    pin = []
    for j in (2, 1, 3):
        ps[j - 1] = (coeff_third * dot(ng[up(a, j)].reshape(2 * Q, A), strips, NT)).astype(bf16)
        pin.append(send(ps.at[j - 1], pr.at[j - 1], at(a=up(a, j)), pr.at[j - 1]))
    xin[2] = over_x(zp.at[up1], up1)
    xin[3] = over_x(zp.at[far], far)
    want = lax.broadcasted_iota(jnp.int32, (2 * Q, A), 0)
    place = lax.broadcasted_iota(jnp.int32, (2 * Q, A), 1)
    inside = want % Q
    hot = (place == b * R + (want // Q) * H + d * Q + inside) & (inside < H - d * Q)
    hot = jnp.where(hot, 1.0, 0.0).astype(bf16)
    own = coeff_third * dot(ng[a].reshape(2 * Q, A), strips, NT) + coeff_second * dot(hot, strips, NT)
    arrived(1, up3)
    for copy in pin:
        copy.wait_recv()
    pt[c, e, d] = (own + pr[0].astype(f32) + pr[1].astype(f32) + pr[2].astype(f32)).astype(bf16)

    def tile_of(c, d):
        return pt.at[c, e, d]

    tin = {k: send(tile_of(c, d), tile_of(c, d), at(c=up(c, k)), tile_of(up(c, 4 - k), d)) for k in (1, 2, 3)}
    tyin = {}
    for k in (0, 1, 2, 3):
        src = up(c, 4 - k)
        if k:
            tin[k].wait_recv()
        tyin[k] = [
            send(tile_of(src, d), tile_of(src, d), at(d=up(d, j)), tile_of(src, up(d, 4 - j))) for j in (1, 3, 2)
        ]

    def product(z, h):
        return dot(pt[z, h].reshape(8 * Q, 16 * Q), xr[z, h].reshape(16 * Q, K), NN)

    arrived(2, up1)
    arrived(3, far)
    tcin = {}
    for k in (0, 1, 2, 3):
        src = up(c, 4 - k)
        for copy in tyin[k]:
            copy.wait_recv()
        tcin[k] = send(pt.at[src, e], pt.at[src, e], at(e=f), pt.at[src, f])
        if k:
            uk[...] += product(src, e)
            tcin[k - 1].wait_recv()
            uk[...] += product(up(c, 5 - k), f)
        else:
            uk[...] = product(src, e)
    tcin[3].wait_recv()
    uk[...] += product(up(c, 1), f)
    for h in range(2):
        for j in range(4):
            size = min(Q, H - j * Q)
            rows = slice(h * H + j * Q, h * H + j * Q + size)
            total = uk[(j * 2 + h) * Q : (j * 2 + h) * Q + size]
            o_ref[rows] = (factor * (coeff_first * x_ref[rows].astype(f32) + total)).astype(bf16)
    for copy in started:
        copy.wait_send()
    for strip in range(4):

        @pl.when(c != strip)
        def _():
            hand(strip).wait_send()


def step(x):
    vmem = pltpu.VMEM
    return pl.pallas_call(
        kernel,
        out_shape=jax.ShapeDtypeStruct((R, K), bf16),
        in_specs=[pl.BlockSpec(memory_space=pltpu.HBM)],
        out_specs=pl.BlockSpec(memory_space=vmem),
        scratch_shapes=[
            vmem((R, K), bf16),
            vmem((H, 2 * K), bf16),
            vmem((4, 4, H, 2 * K), bf16),
            vmem((4, H, 2 * K), bf16),
            vmem((4, 2, 4, 4 * Q, K), bf16),
            vmem((4, 2, H, K), bf16),
            vmem((4, 4, Q, A), f32),
            vmem((4, H, A), bf16),
            vmem((4, H, A), bf16),
            vmem((4, 4, Q, A), bf16),
            vmem((4, 4, Q, A), bf16),
            vmem((Q, A), f32),
            vmem((Q, A), bf16),
            vmem((4, Q, A), bf16),
            vmem((4, Q, A), bf16),
            vmem((4, 4, Q, A), bf16),
            vmem((4, 2, Q, A), bf16),
            vmem((3, 2 * Q, 16 * Q), bf16),
            vmem((3, 2 * Q, 16 * Q), bf16),
            vmem((4, 2, 4, 2 * Q, 16 * Q), bf16),
            vmem((8 * Q, K), f32),
            pltpu.SemaphoreType.DMA,
            pltpu.SemaphoreType.DMA((128,)),
            pltpu.SemaphoreType.DMA((128,)),
        ],
        compiler_params=pltpu.CompilerParams(
            collective_id=0, has_side_effects=True, vmem_limit_bytes=44 << 20
        ),
        cost_estimate=pl.CostEstimate(flops=2 * 10**9, bytes_accessed=520000, transcendentals=0),
        name="newton_schulz",
    )(x)


def solution(mesh):
    return jax.shard_map(
        step, mesh=mesh, in_specs=(P("row", "col"),), out_specs=P("row", "col"), check_vma=False
    )
```

```python
import functools
import math

import jax
import jax.numpy as jnp
from jax import lax
from jax.experimental import pallas as pl
from jax.experimental.pallas import tpu as pltpu
from jax.sharding import PartitionSpec as P

MESH = pl.DeviceIdType.MESH
ROWS = 3584
COLS = 18432
R = 224
H = 112
K = 576
A = 896
Q = 32
bf16 = jnp.bfloat16
f32 = jnp.float32

coeff_first = 3.4445
coeff_second = -4.775
coeff_third = 2.0315
factor = 0.2 * math.sqrt(max(ROWS, COLS))

NN = (((1,), (0,)), ((), ()))
NT = (((1,), (1,)), ((), ()))


def dot(x, y, dims):
    return lax.dot_general(x, y, dims, preferred_element_type=f32)


def kernel(
    x_hbm,
    o_ref,
    x_ref,
    xp,
    ap,
    zp,
    xr,
    xa,
    gk,
    gs,
    gr,
    ys,
    yr,
    yk,
    zk,
    zs,
    zr,
    mg,
    ng,
    ps,
    pr,
    pt,
    uk,
    ls,
    ss,
    rs,
):
    row, col = lax.axis_index("row"), lax.axis_index("col")
    a, b = row // 4, row % 4
    c, d, e = col // 8, (col // 2) % 4, col % 2
    f = 1 - e

    def at(a=a, b=b, c=c, d=d, e=e):
        return (a * 4 + b, c * 8 + d * 2 + e)

    def up(v, k):
        return (v + k) % 4

    fetch = pltpu.make_async_copy(x_hbm, x_ref, ls)
    fetch.start()

    barrier = pltpu.get_barrier_semaphore()
    friends = [at(e=f)]
    for k in range(1, 4):
        friends += [at(a=up(a, k)), at(b=up(b, k)), at(c=up(c, k)), at(d=up(d, k))]
    for friend in friends:
        pl.semaphore_signal(barrier, inc=1, device_id=friend, device_id_type=MESH)
    fetch.wait()
    xp[:, :K] = x_ref[:H]
    xp[:, K:] = x_ref[H:]
    pl.semaphore_wait(barrier, len(friends))

    started = []
    count = [4]

    def remote(src, dst, to, s, r):
        return pltpu.make_async_remote_copy(
            src_ref=src, dst_ref=dst, send_sem=ss.at[s], recv_sem=rs.at[r], device_id=to, device_id_type=MESH
        )

    def send(src, dst, to, landing):
        n = count[0]
        count[0] += 1
        copy = remote(src, dst, to, n, n)
        copy.start()
        started.append(copy)
        return remote(src, landing, to, n, n)

    piece = (pl.ds(0, 64), pl.ds(64, H - 64))
    up1, up3, far = up(a, 1), up(a, 3), up(a, 2)
    fwd, bwd = {}, {}
    for n in range(2):
        here = xp.at[piece[n]]
        fwd[n] = send(here, zp.at[a, piece[n]], at(a=up1), zp.at[up3, piece[n]])
        here = xp.at[piece[1 - n]]
        bwd[1 - n] = send(here, zp.at[a, piece[1 - n]], at(a=up3), zp.at[up1, piece[1 - n]])

    def over_x(src, plane):
        return {k: send(src, ap.at[plane, b], at(b=up(b, k)), ap.at[plane, up(b, 4 - k)]) for k in (2, 1, 3)}

    xin = {0: over_x(xp, a)}

    xr[:, :, :, H:] = jnp.zeros((4, 2, 4, 4 * Q - H, K), bf16)
    gk[:, 3, 16:] = jnp.zeros((4, 16, A), f32)
    ys[:, 3, 16:] = jnp.zeros((4, 16, A), bf16)

    def spread(packed, plane, place):
        xr[plane, 0, place, :H] = packed[:, :K]
        xr[plane, 1, place, :H] = packed[:, K:]

    def arrived(n, plane):
        for k in (2, 1, 3):
            xin[n][k].wait_recv()
            spread(ap[plane, up(b, 4 - k)], plane, up(b, 4 - k))

    for h in range(2):
        xr[a, h, b, :H] = x_ref[h * H : (h + 1) * H]
    arrived(0, a)
    for v in range(4):
        for h in range(2):
            xa[v, h] = xr[a, h, v, :H]

    cin, yin = {}, {}

    def gram(n, strip):
        right = xa[...].reshape(A, K)
        gs[strip] = dot(xr[strip, f, b, :H], right, NT).astype(bf16)
        cin[n] = send(gs.at[strip], gr.at[strip], at(e=f), gr.at[strip])
        part = dot(xr[strip, e, b, :H], right, NT)
        for j in range(4):
            size = min(Q, H - j * Q)
            gk[strip, j, :size] = part[j * Q : j * Q + size]

    def combine(n, strip):
        cin[n].wait_recv()
        for j in range(4):
            size = min(Q, H - j * Q)
            both = gk[strip, j, :size] + gr[strip, j * Q : j * Q + size].astype(f32)
            gk[strip, j, :size] = both
            ys[strip, j, :size] = both.astype(bf16)
        yin[n] = [
            send(ys.at[strip, up(d, k)], yr.at[strip, d], at(d=up(d, k)), yr.at[strip, up(d, 4 - k)]) for k in (2, 1, 3)
        ]

    def hand(strip):
        return remote(zs.at[strip], zr.at[c], at(c=strip), strip, c)

    def pass_on(n, strip):
        for copy in yin[n]:
            copy.wait_recv()
        total = gk[strip, d] + sum(yr[strip, up(d, k)].astype(f32) for k in (1, 2, 3))

        @pl.when(strip == c)
        def _():
            yk[...] = total

        @pl.when(strip != c)
        def _():
            zs[strip] = total.astype(bf16)
            hand(strip).start()

    gram(0, a)
    fwd[0].wait_recv()
    far0 = send(zp.at[up3, piece[0]], zp.at[up3, piece[0]], at(a=up1), zp.at[far, piece[0]])
    bwd[1].wait_recv()
    far1 = send(zp.at[up1, piece[1]], zp.at[up1, piece[1]], at(a=up3), zp.at[far, piece[1]])
    combine(0, a)
    fwd[1].wait_recv()
    xin[1] = over_x(zp.at[up3], up3)
    spread(zp[up3], up3, b)
    gram(1, up3)
    bwd[0].wait_recv()
    spread(zp[up1], up1, b)
    gram(2, up1)
    combine(1, up3)
    combine(2, up1)
    pass_on(0, a)
    far0.wait_recv()
    far1.wait_recv()
    spread(zp[far], far, b)
    gram(3, far)
    combine(3, far)
    pass_on(1, up3)
    pass_on(2, up1)
    pass_on(3, far)
    for k in (1, 2, 3):
        remote(zs.at[c], zr.at[up(c, k)], at(c=up(c, k)), c, up(c, k)).wait_recv()
    zk[...] = (yk[...] + sum(zr[up(c, k)].astype(f32) for k in (1, 2, 3))).astype(bf16)

    top, low = pl.ds(0, 16), pl.ds(16, 16)
    min_ = [send(zk.at[top], mg.at[b, d, top], at(b=up(b, k)), mg.at[up(b, 4 - k), d, top]) for k in (2, 1, 3)]
    myin = [send(zk.at[low], mg.at[b, d, low], at(d=up(d, k)), mg.at[b, up(d, 4 - k), low]) for k in (2, 1, 3)]
    nin = [send(zk, ng.at[c, e], at(c=up(c, k)), ng.at[up(c, 4 - k), e]) for k in (1, 2, 3)]
    mg[b, d] = zk[...]
    ng[c, e] = zk[...]
    for copy in min_:
        copy.wait_recv()
    m2in = [send(mg.at[:, d, top], mg.at[:, d, top], at(d=up(d, k)), mg.at[:, up(d, 4 - k), top]) for k in (2, 1, 3)]
    for copy in myin:
        copy.wait_recv()
    m2in += [send(mg.at[b, :, low], mg.at[b, :, low], at(b=up(b, k)), mg.at[up(b, 4 - k), :, low]) for k in (2, 1, 3)]
    for copy in nin:
        copy.wait_recv()
    ncore = send(ng.at[:, e], ng.at[:, e], at(e=f), ng.at[:, f])
    for copy in m2in + [ncore]:
        copy.wait_recv()

    strips = mg[...].reshape(16 * Q, A)
    pin = []
    for j in (2, 1, 3):
        ps[j - 1] = (coeff_third * dot(ng[up(a, j)].reshape(2 * Q, A), strips, NT)).astype(bf16)
        pin.append(send(ps.at[j - 1], pr.at[j - 1], at(a=up(a, j)), pr.at[j - 1]))
    xin[2] = over_x(zp.at[up1], up1)
    xin[3] = over_x(zp.at[far], far)
    want = lax.broadcasted_iota(jnp.int32, (2 * Q, A), 0)
    place = lax.broadcasted_iota(jnp.int32, (2 * Q, A), 1)
    inside = want % Q
    hot = (place == b * R + (want // Q) * H + d * Q + inside) & (inside < H - d * Q)
    hot = jnp.where(hot, 1.0, 0.0).astype(bf16)
    own = coeff_third * dot(ng[a].reshape(2 * Q, A), strips, NT) + coeff_second * dot(hot, strips, NT)
    arrived(1, up3)
    for copy in pin:
        copy.wait_recv()
    pt[c, e, d] = (own + pr[0].astype(f32) + pr[1].astype(f32) + pr[2].astype(f32)).astype(bf16)

    def tile_of(c, d):
        return pt.at[c, e, d]

    tin = {k: send(tile_of(c, d), tile_of(c, d), at(c=up(c, k)), tile_of(up(c, 4 - k), d)) for k in (1, 2, 3)}
    tyin = {}
    for k in (0, 1, 2, 3):
        src = up(c, 4 - k)
        if k:
            tin[k].wait_recv()
        tyin[k] = [
            send(tile_of(src, d), tile_of(src, d), at(d=up(d, j)), tile_of(src, up(d, 4 - j))) for j in (2, 1, 3)
        ]

    def product(z, h):
        return dot(pt[z, h].reshape(8 * Q, 16 * Q), xr[z, h].reshape(16 * Q, K), NN)

    arrived(2, up1)
    arrived(3, far)
    tcin = {}
    for k in (0, 1, 2, 3):
        src = up(c, 4 - k)
        for copy in tyin[k]:
            copy.wait_recv()
        tcin[k] = send(pt.at[src, e], pt.at[src, e], at(e=f), pt.at[src, f])
        if k:
            uk[...] += product(src, e)
            tcin[k - 1].wait_recv()
            uk[...] += product(up(c, 5 - k), f)
        else:
            uk[...] = product(src, e)
    tcin[3].wait_recv()
    uk[...] += product(up(c, 1), f)
    for h in range(2):
        for j in range(4):
            size = min(Q, H - j * Q)
            rows = slice(h * H + j * Q, h * H + j * Q + size)
            total = uk[(j * 2 + h) * Q : (j * 2 + h) * Q + size]
            o_ref[rows] = (factor * (coeff_first * x_ref[rows].astype(f32) + total)).astype(bf16)
    for copy in started:
        copy.wait_send()
    for strip in range(4):

        @pl.when(c != strip)
        def _():
            hand(strip).wait_send()


def step(x):
    vmem = pltpu.VMEM
    return pl.pallas_call(
        kernel,
        out_shape=jax.ShapeDtypeStruct((R, K), bf16),
        in_specs=[pl.BlockSpec(memory_space=pltpu.HBM)],
        out_specs=pl.BlockSpec(memory_space=vmem),
        scratch_shapes=[
            vmem((R, K), bf16),
            vmem((H, 2 * K), bf16),
            vmem((4, 4, H, 2 * K), bf16),
            vmem((4, H, 2 * K), bf16),
            vmem((4, 2, 4, 4 * Q, K), bf16),
            vmem((4, 2, H, K), bf16),
            vmem((4, 4, Q, A), f32),
            vmem((4, H, A), bf16),
            vmem((4, H, A), bf16),
            vmem((4, 4, Q, A), bf16),
            vmem((4, 4, Q, A), bf16),
            vmem((Q, A), f32),
            vmem((Q, A), bf16),
            vmem((4, Q, A), bf16),
            vmem((4, Q, A), bf16),
            vmem((4, 4, Q, A), bf16),
            vmem((4, 2, Q, A), bf16),
            vmem((3, 2 * Q, 16 * Q), bf16),
            vmem((3, 2 * Q, 16 * Q), bf16),
            vmem((4, 2, 4, 2 * Q, 16 * Q), bf16),
            vmem((8 * Q, K), f32),
            pltpu.SemaphoreType.DMA,
            pltpu.SemaphoreType.DMA((128,)),
            pltpu.SemaphoreType.DMA((128,)),
        ],
        compiler_params=pltpu.CompilerParams(
            collective_id=0, has_side_effects=True, vmem_limit_bytes=44 << 20
        ),
        cost_estimate=pl.CostEstimate(flops=2 * 10**9, bytes_accessed=520000, transcendentals=0),
        name="newton_schulz",
    )(x)


def solution(mesh):
    return jax.shard_map(
        step, mesh=mesh, in_specs=(P("row", "col"),), out_specs=P("row", "col"), check_vma=False
    )
```
